256 devices in a mesh: gx: 16 (over y, x_lo, core), gy: 16 (over z, x_hi).
Axes of the slice: x: 4 (x_hi: 2, x_lo: 2; x = x_hi * 2 + x_lo), y: 4, z: 8, core: 2. Of those that a mesh axis runs over, the one named last changes fastest.
Arguments:
- start_state: float32 [2, 8, 2, 128, 2048], P(None, None, None, 'gx', 'gy'), may hold values from -6 to 6
- probe_state: float32 [2, 8, 2, 128, 2048], P(None, None, None, 'gx', 'gy'), may hold values from -6 to 6
- hop_offsets: int32 [10, 2, 128, 2048], P(None, None, 'gx', 'gy'), may hold values from 0 to 24, as said below
- hop_orbitals: int32 [10, 2, 128, 2048], P(None, None, 'gx', 'gy'), may hold values from 0 to 1, as said below
- hop_index: int32 [10, 2, 128, 2048], P(None, None, 'gx', 'gy'), may hold values from 0 to 63, as said below
- orbital_type: int32 [2, 128, 2048], P(None, 'gx', 'gy'), may hold values from 0 to 3
- hop_table: float32 [64], replicated, may hold values from -0.09 to -0.045
- onsite_table: float32 [4], replicated, may hold values from -0.1 to 0.1
Outputs:
- final_state: float32 [2, 8, 2, 128, 2048], P(None, None, None, 'gx', 'gy')
- intersections: float32 [4, 2, 8], replicated
The draws below stay inside these ranges and needn't reach their ends.
Inputs may be any that keep to these rules, and one draw needn't show every extreme that they name: `hop_offsets`: a code o stands for the offset (o // 5 - 2, o % 5 - 2) in cells along x and y; hoppings come in mirrored pairs: if hopping k into orbital a of cell (x, y) comes from orbital b of the cell at offset (p, q), then hopping k into orbital b of that cell comes from orbital a of cell (x, y), with offset (-p, -q) and the same hop_index entry. `hop_orbitals`: the source orbital is the receiving orbital where the two components of the offset add up to an odd number, and the other orbital where they add up to an even number. `hop_index`: a hopping and its mirrored partner name the same entry.
All inputs are finite; a program needn't handle non-finite values.
Results may differ from the reference program's by a relative error of at most 0.0001.
Values sent between devices are 32-bit elements; how exact they have to be, the bound alone decides.
No kernel may reach another device: no remote copies, remote signals or barrier semaphores. Data moves between devices by JAX's collectives and lax.ppermute only.
A program may use at most 128 MiB of HBM per device.

```python
import math
import jax
import jax.numpy as jnp
from jax import lax

ORB = 2
VEC = 8
NB = 10
NTAB = 64
NTYPE = 4
APPLY = 4
STEPS = 4
NX = 128
NY = 2048


def pair_lines(key, along, across):
    step_key, shift_key, flag_key, entry_key = jax.random.split(key, 4)
    row_ids = jnp.arange(along, dtype=jnp.int32)[:, None]
    place_ids = jnp.arange(across, dtype=jnp.int32)[None, :]
    band_step = 1 + jax.random.randint(step_key, (along // 4,), 0, 2, dtype=jnp.int32)
    stride = jnp.repeat(band_step, 4)[:, None]
    anchored = row_ids // stride % 2 == 0
    cross_shift = jax.random.randint(shift_key, (along,), -1, 2, dtype=jnp.int32)
    flip_flags = jnp.repeat(jax.random.randint(flag_key, (along, across // 2), 0, 2, dtype=jnp.int32), 2, axis=1)
    entries = jax.random.randint(entry_key, (ORB, along, across), 0, NTAB, dtype=jnp.int32)
    forward = cross_shift[:, None] + flip_flags * (1 - 2 * (place_ids % 2))
    partner = (row_ids - stride) % along
    partner_full = jnp.broadcast_to(partner, (along, across))
    partner_shift = cross_shift[partner_full]
    reduced = (place_ids - partner_shift) % across
    partner_flag = flip_flags[partner_full, reduced]
    mirror = reduced + partner_flag * (1 - 2 * (reduced % 2))
    backward = partner_shift + partner_flag * (1 - 2 * (mirror % 2))
    step_along = jnp.where(anchored, stride, -stride)
    step_across = jnp.where(anchored, forward, -backward)
    orbit_ids = jnp.arange(ORB, dtype=jnp.int32)[:, None, None]
    parity = (step_along + step_across) % 2
    source = jnp.where(parity[None] == 1, orbit_ids, 1 - orbit_ids)
    near_entry = entries
    far_entry = entries[source, partner_full[None], mirror[None]]
    chosen = jnp.where(anchored[None], near_entry, far_entry)
    return (step_along, step_across, source.astype(jnp.int32), chosen.astype(jnp.int32))


def hop_structure(key):
    key = jax.random.fold_in(key, 17)
    offset_list = []
    orbital_list = []
    entry_list = []
    for number in range(NB):
        slot_key = jax.random.fold_in(key, number)
        axis_key, row_key, column_key = jax.random.split(slot_key, 3)
        along_x = jax.random.randint(axis_key, (), 0, 2, dtype=jnp.int32) == 0
        xa_step, xa_cross, xa_source, xa_entry = pair_lines(row_key, NX, NY)
        ya_step, ya_cross, ya_source, ya_entry = pair_lines(column_key, NY, NX)
        shift_x = jnp.where(along_x, xa_step, ya_cross.T)
        shift_y = jnp.where(along_x, xa_cross, ya_step.T)
        source = jnp.where(along_x, xa_source, jnp.transpose(ya_source, (0, 2, 1)))
        entry = jnp.where(along_x, xa_entry, jnp.transpose(ya_entry, (0, 2, 1)))
        offset_code = (shift_x + 2) * 5 + (shift_y + 2)
        offset_list.append(jnp.broadcast_to(offset_code[None], (ORB, NX, NY)))
        orbital_list.append(source)
        entry_list.append(entry)
    return (jnp.stack(offset_list).astype(jnp.int32), jnp.stack(orbital_list).astype(jnp.int32), jnp.stack(entry_list).astype(jnp.int32))


def draw_hop_offsets(key, part):
    return hop_structure(key)[0]


def draw_hop_orbitals(key, part):
    return hop_structure(key)[1]


def draw_hop_index(key, part):
    return hop_structure(key)[2]


def touch_ends(drawn, rng, low, largest):
    shape = drawn.shape
    index_at = [jax.random.randint(jax.random.fold_in(rng, axis), (), 0, shape[axis]) for axis in range(len(shape))]
    drawn = drawn.at[tuple(index_at)].set(low)
    longest = shape.index(max(shape))
    index_at[longest] = (index_at[longest] + 1) % shape[longest]
    return drawn.at[tuple(index_at)].set(largest)


def levels(stream_key, extent, pieces, smallest, high):
    factor_of = 1.0
    for axis_at, parts in pieces:
        draws = jax.random.uniform(jax.random.fold_in(jax.random.fold_in(stream_key, 6), axis_at), (parts,), jnp.float32, smallest / len(pieces), high / len(pieces))
        factor_of = factor_of * jnp.repeat(jnp.exp(draws), extent[axis_at] // parts).reshape((-1,) + (1,) * (len(extent) - 1 - axis_at))
    return factor_of


def normal_values(rng, dims, scale, reach, cuts=(), kind=jnp.bfloat16):
    values = scale * jax.random.normal(rng, dims, jnp.float32)
    if cuts:
        values = values * levels(rng, dims, cuts, -0.22, 0.18)
    return jnp.clip(values, -reach, reach).astype(kind)


def setup_inputs(seed: int = 0) -> dict:
    arg_keys = jax.random.split(jax.random.key(seed), 9)
    start_state = normal_values(arg_keys[0], (2, VEC, ORB, NX, NY), 1.0, 6.0, ((3, 16), (4, 16)), jnp.float32)
    probe_state = normal_values(arg_keys[1], (2, VEC, ORB, NX, NY), 1.0, 6.0, ((3, 16), (4, 16)), jnp.float32)
    hop_offsets = draw_hop_offsets(jax.random.fold_in(arg_keys[8], 71), 0)
    hop_orbitals = draw_hop_orbitals(jax.random.fold_in(arg_keys[8], 71), 0)
    hop_index = draw_hop_index(jax.random.fold_in(arg_keys[8], 71), 0)
    orbital_type = touch_ends(jax.random.randint(arg_keys[5], (ORB, NX, NY), 0, NTYPE), jax.random.fold_in(arg_keys[5], 1), 0, NTYPE - 1).astype(jnp.int32)
    hop_table = jnp.clip(jax.random.uniform(arg_keys[6], (NTAB,), jnp.float32, -0.09, -0.045), -0.09, -0.045)
    onsite_table = jnp.clip(jax.random.uniform(arg_keys[7], (NTYPE,), jnp.float32, -0.1, 0.1), -0.1, 0.1)
    return dict(start_state=start_state, probe_state=probe_state, hop_offsets=hop_offsets, hop_orbitals=hop_orbitals, hop_index=hop_index, orbital_type=orbital_type, hop_table=hop_table, onsite_table=onsite_table)


time_step = 2.6

def bessel(order, arg):
    total = 0.0
    for term in range(40):
        total += (-1.0) ** term * (arg / 2.0) ** (2 * term + order) / (math.factorial(term) * math.factorial(term + order))
    return total

def weights(count):
    real_part = []
    imag_part = []
    phases = [(1.0, 0.0), (0.0, -1.0), (-1.0, 0.0), (0.0, 1.0)]
    for order in range(count + 1):
        scale = bessel(order, time_step) * (1.0 if order == 0 else 2.0)
        real_part.append(scale * phases[order % 4][0])
        imag_part.append(scale * phases[order % 4][1])
    return (real_part, imag_part)

def add_term(accum, term, order, real_part, imag_part):
    half = term.shape[0] // 2
    rotated = jnp.concatenate([-term[half:], term[:half]], axis=0)
    return accum + real_part[order] * term + imag_part[order] * rotated

def reference(start_state, probe_state, hop_offsets, hop_orbitals, hop_index, orbital_type, hop_table, onsite_table):
    xs = jnp.arange(NX, dtype=jnp.int32)[None, :, None]
    ys = jnp.arange(NY, dtype=jnp.int32)[None, None, :]
    sources = []
    values = []
    for slot in range(NB):
        shift_x = hop_offsets[slot] // 5 - 2
        shift_y = hop_offsets[slot] % 5 - 2
        source = (hop_orbitals[slot] * NX + (xs + shift_x) % NX) * NY + (ys + shift_y) % NY
        sources.append(source.reshape(-1).astype(jnp.int32))
        values.append(hop_table[hop_index[slot]].reshape(1, -1))
    onsite = onsite_table[orbital_type].reshape(1, -1)

    def apply_hops(field):
        total = onsite * field
        for slot in range(NB):
            total = total + values[slot] * field[:, sources[slot]]
        return total
    real_part, imag_part = weights(APPLY)
    state = start_state.reshape(2 * VEC, -1)
    probe = probe_state.reshape(2 * VEC, -1)
    norm = 1.0 / math.sqrt(2.0 * ORB * NX * NY)
    results = []
    for step in range(STEPS):
        accum = add_term(jnp.zeros_like(state), state, 0, real_part, imag_part)
        previous = state
        current = apply_hops(state)
        accum = add_term(accum, current, 1, real_part, imag_part)
        for order in range(2, APPLY + 1):
            following = 2.0 * apply_hops(current) - previous
            previous, current = (current, following)
            accum = add_term(accum, current, order, real_part, imag_part)
        state = accum
        real_sum = lax.optimization_barrier(jnp.sum(probe[:VEC] * state[:VEC] + probe[VEC:] * state[VEC:], axis=1))
        imag_sum = lax.optimization_barrier(jnp.sum(probe[:VEC] * state[VEC:] - probe[VEC:] * state[:VEC], axis=1))
        results.append(jnp.stack([real_sum, imag_sum]) * norm)
    final_state = state.reshape(2, VEC, ORB, NX, NY)
    return (final_state, jnp.stack(results))
```

```python
import functools
import math

import jax
import jax.numpy as jnp
from jax import lax
from jax.experimental import pallas as pl
from jax.experimental.pallas import tpu as pltpu
from jax.sharding import PartitionSpec as P

APPLY = 4
STEPS = 4
TIME_STEP = 2.6

ROWS = 8
LANES = 128
EDGE = 32
REGION = 3 * ROWS
TILES = 3
VMEM_LIMIT = 48 * 1024 * 1024

HALF = [(p, q) for p in range(3) for q in range(-2, 3) if p > 0 or q > 0]
CROSS = 2 * len(HALF)
ONSITE = CROSS + 1
KINDS = ONSITE + 2
SHIFTED = [(number, half) for number, half in enumerate(HALF) if half[1] != 0]
SHIFT_SLOT = {half: 2 * place for place, (_, half) in enumerate(SHIFTED)}
COEF_ROWS = KINDS + 2 * len(SHIFTED)


def bessel(order, arg):
    total = 0.0
    for term in range(40):
        total += (
            (-1.0) ** term
            * (arg / 2.0) ** (2 * term + order)
            / (math.factorial(term) * math.factorial(term + order))
        )
    return total


def roll(tile, amount):
    amount = amount % LANES
    return tile if amount == 0 else pltpu.roll(tile, amount, 1)


def lane_ids():
    return lax.broadcasted_iota(jnp.int32, (ROWS, LANES), 1)


def shift_tiles(tiles, amount, lanes):
    even, odd, tail = (roll(tile, amount) for tile in tiles)
    if amount > 0:
        tail = jnp.where(lanes < amount, even, tail)
        tail = jnp.where((lanes >= 64) & (lanes < 64 + amount), odd, tail)
    else:
        even = jnp.where(lanes >= LANES + amount, tail, even)
        odd = jnp.where((lanes >= 64 + amount) & (lanes < 64), tail, odd)
    return even, odd, tail


def in_group(lanes, group):
    return (lanes >= EDGE * group) & (lanes < EDGE * (group + 1))


def turned(real, imag):
    return roll(real, EDGE), roll(imag, EDGE + 64)


def pack_kernel(vectors, slots, state, offsets, index, kinds, hop_table, onsite_table, coef, to_right, to_left):
    lanes = lane_ids()
    low = lanes < 64
    first = in_group(lanes, 0) | in_group(lanes, 2)
    for v in range(vectors):
        strips = []
        for a in range(2):
            real, imag = turned(state[0, v, a], state[1, v, a])
            strips.append(jnp.where(low, real, imag))
        to_right[v] = jnp.where(first, strips[0], roll(strips[1], EDGE))
        to_left[v] = jnp.where(first, roll(strips[1], -EDGE), strips[0])
    table = jnp.broadcast_to(hop_table[...], (ROWS, LANES))
    levels = jnp.broadcast_to(onsite_table[...], (ROWS, LANES))
    arrays = [jnp.zeros((ROWS, LANES), jnp.float32) for _ in range(KINDS)]
    for a in range(2):
        for slot in range(slots):
            amount = jnp.take_along_axis(table, index[slot, a], axis=1)
            code = offsets[slot, a]
            for number, (p, q) in enumerate(HALF):
                at = 2 * number + a
                arrays[at] = arrays[at] + jnp.where(code == 5 * (p + 2) + q + 2, amount, 0.0)
            if a == 0:
                arrays[CROSS] = arrays[CROSS] + jnp.where(code == 12, amount, 0.0)
        arrays[ONSITE + a] = jnp.take_along_axis(levels, kinds[a], axis=1)
    for start in range(0, KINDS, 4):
        right = left = None
        for group in range(min(4, KINDS - start)):
            double = 2.0 * arrays[start + group]
            coef[start + group] = double
            base = roll(double, EDGE)
            from_tail = roll(base, EDGE * group)
            from_head = roll(base, EDGE * (group - 1))
            right = from_tail if right is None else jnp.where(in_group(lanes, group), from_tail, right)
            left = from_head if left is None else jnp.where(in_group(lanes, group), from_head, left)
        to_right[vectors + start // 4] = right
        to_left[vectors + start // 4] = left


def widen_kernel(vectors, state, coef, from_left, from_right, wide):
    lanes = lane_ids()
    groups = [in_group(lanes, g) for g in range(4)]
    for v in range(vectors):
        for a in range(2):
            real, imag = turned(state[0, v, a], state[1, v, a])
            left = roll(from_left[v], -EDGE * a)
            right = roll(from_right[v], EDGE * a)
            at = (2 * v + a) * TILES
            wide[at] = jnp.where(groups[0], left, real)
            wide[at + 1] = jnp.where(groups[2], left, imag)
            wide[at + 2] = jnp.where(groups[0], real, jnp.where(groups[2], imag, right))
    base = 2 * vectors * TILES
    for pair in range(0, KINDS, 2):
        tails = None
        for j in range(pair, min(pair + 2, KINDS)):
            group = j % 4
            body = roll(coef[j], EDGE)
            left = roll(from_left[vectors + j // 4], -EDGE * group)
            right = roll(from_right[vectors + j // 4], EDGE * (1 - group))
            wide[base + j] = jnp.where(groups[0], left, body)
            tail = jnp.where(groups[0], body, right)
            tails = tail if tails is None else jnp.where(lanes < 64, tails, roll(tail, 64))
        wide[base + KINDS + pair // 2] = tails


def spread_coefficients(base, blocks, coefs):
    lanes = lane_ids()
    low = lanes < 64
    for part, block in enumerate(blocks):
        rows = pl.ds(ROWS * part, ROWS)
        for j in range(KINDS):
            even = block[base + j]
            odd = roll(even, 64)
            tail = block[base + KINDS + j // 2]
            other = roll(tail, 64)
            tail = jnp.where(low, tail, other) if j % 2 == 0 else jnp.where(low, other, tail)
            tiles = (even, odd, tail)
            for t in range(TILES):
                coefs[TILES * j + t, rows, :] = tiles[t]
            if j < CROSS and HALF[j // 2][1] != 0:
                moved = shift_tiles(tiles, HALF[j // 2][1], lanes)
                at = KINDS + SHIFT_SLOT[HALF[j // 2]] + j % 2
                for t in range(TILES):
                    coefs[TILES * at + t, rows, :] = moved[t]


def coefficient(coefs, dx, dy, a, t, top):
    source = a if (dx + dy) % 2 else 1 - a
    if (dx, dy) == (0, 0):
        at, row = CROSS, top
    elif (dx, dy) in HALF:
        at = KINDS + SHIFT_SLOT[(dx, dy)] + a if dy else 2 * HALF.index((dx, dy)) + a
        row = top
    else:
        at, row = 2 * HALF.index((-dx, -dy)) + source, top + dx
    return source, coefs[TILES * at + t, pl.ds(row, ROWS), :]


def apply_twice(field, coefs, a, group, width, top, lanes):
    sums = [[[None] * 5 for _ in range(TILES)] for _ in range(width)]
    for dx in range(-2, 3):
        rows = pl.ds(top + dx, ROWS)
        for t in range(TILES):
            values = [
                [field[((group * width + w) * 2 + b) * TILES + t, rows, :] for b in range(2)]
                for w in range(width)
            ]
            for dy in range(-2, 3):
                source, factor = coefficient(coefs, dx, dy, a, t, top)
                for w in range(width):
                    term = factor * values[w][source]
                    old = sums[w][t][dy + 2]
                    sums[w][t][dy + 2] = term if old is None else old + term
            if dx == 0:
                factor = coefs[TILES * (ONSITE + a) + t, pl.ds(top, ROWS), :]
                for w in range(width):
                    sums[w][t][2] = sums[w][t][2] + factor * values[w][a]
    results = []
    for w in range(width):
        total = [sums[w][t][2] for t in range(TILES)]
        for dy in (-2, -1, 1, 2):
            moved = shift_tiles([sums[w][t][dy + 2] for t in range(TILES)], -dy, lanes)
            total = [total[t] + moved[t] for t in range(TILES)]
        results.append(total)
    return results


def time_step(vectors, width, coefs, probe, terms, products, finish):
    lanes = lane_ids()
    scale = [bessel(order, TIME_STEP) * (1.0 if order == 0 else 2.0) for order in range(APPLY + 1)]
    for order in range(1, APPLY + 1):
        low, high = 2 * order, REGION - 2 * order
        tops = list(range(low, high - ROWS + 1, ROWS))
        if tops[-1] != high - ROWS:
            tops.append(high - ROWS)
        for a in range(2):

            def body(group, carry):
                for top in tops:
                    images = apply_twice(terms[order - 1], coefs, a, group, width, top, lanes)
                    for w in range(width):
                        v = group * width + w
                        at = (2 * v + a) * TILES
                        rows = pl.ds(top, ROWS)
                        if order == 1:
                            new = [0.5 * images[w][t] for t in range(TILES)]
                        else:
                            new = [images[w][t] - terms[order - 2][at + t, rows, :] for t in range(TILES)]
                        if order < APPLY:
                            for t in range(TILES):
                                terms[order][at + t, rows, :] = new[t]
                            continue
                        even = []
                        odd = []
                        for t in range(TILES):
                            part = [terms[k][at + t, rows, :] for k in range(APPLY)]
                            even.append(scale[0] * part[0] - scale[2] * part[2] + scale[4] * new[t])
                            odd.append(roll(scale[1] * part[1] - scale[3] * part[3], 64))
                        real = even[0] + odd[1]
                        imag = even[1] - odd[0]
                        tail = even[2] + jnp.where(lanes < 64, odd[2], -odd[2])
                        own_real = roll(jnp.where(in_group(lanes, 0), tail, real), -EDGE)
                        own_imag = roll(jnp.where(in_group(lanes, 2), tail, imag), -EDGE - 64)
                        probe_real, probe_imag = probe[0, v, a], probe[1, v, a]
                        same = probe_real * own_real + probe_imag * own_imag
                        cross = probe_real * own_imag - probe_imag * own_real
                        if a == 1:
                            same = same + products[v]
                            cross = cross + products[vectors + v]
                        products[v] = same
                        products[vectors + v] = cross
                        finish(at, v, a, (real, imag, tail), (own_real, own_imag))
                return carry

            lax.fori_loop(0, vectors // width, body, 0)


def probe_row(products):
    count = products.shape[0]
    sums = jnp.sum(jnp.sum(products[...], axis=1), axis=1, keepdims=True)
    rows = lax.broadcasted_iota(jnp.int32, (count, LANES), 0)
    lanes = lax.broadcasted_iota(jnp.int32, (count, LANES), 1)
    return jnp.sum(jnp.where(rows == lanes, sums, 0.0), axis=0, keepdims=True)


def gather_rows(vectors, first, own, up, down):
    for part, block in enumerate((up, own, down)):
        for at in range(2 * vectors * TILES):
            first[at, pl.ds(ROWS * part, ROWS), :] = block[at]


def first_kernel(vectors, width, own, up, down, probe, state, coefs, sums, t0, t1, t2, t3, products):
    gather_rows(vectors, t0, own, up, down)
    spread_coefficients(2 * vectors * TILES, (up, own, down), coefs)

    def finish(at, v, a, tiles, cells):
        for t in range(TILES):
            state[at + t] = tiles[t]

    time_step(vectors, width, coefs, probe, (t0, t1, t2, t3), products, finish)
    sums[...] = probe_row(products)


def middle_kernel(vectors, width, own, up, down, coefs, probe, state, sums, t0, t1, t2, t3, products):
    gather_rows(vectors, t0, own, up, down)

    def finish(at, v, a, tiles, cells):
        for t in range(TILES):
            state[at + t] = tiles[t]

    time_step(vectors, width, coefs, probe, (t0, t1, t2, t3), products, finish)
    sums[...] = probe_row(products)


def last_kernel(vectors, width, own, up, down, coefs, probe, s0, s1, s2, state, sums, t0, t1, t2, t3, products):
    gather_rows(vectors, t0, own, up, down)

    def finish(at, v, a, tiles, cells):
        state[0, v, a] = cells[0]
        state[1, v, a] = cells[1]

    time_step(vectors, width, coefs, probe, (t0, t1, t2, t3), products, finish)
    rows = jnp.concatenate([s0[...], s1[...], s2[...], probe_row(products)], axis=0)
    for copy in range(sums.shape[0]):
        sums[copy] = rows


def call(kernel, out_shapes, scratch=()):
    return pl.pallas_call(
        kernel,
        out_shape=[jax.ShapeDtypeStruct(shape, jnp.float32) for shape in out_shapes],
        scratch_shapes=[pltpu.VMEM(shape, jnp.float32) for shape in scratch],
        compiler_params=pltpu.CompilerParams(vmem_limit_bytes=VMEM_LIMIT),
    )


def neighbours(block, axis):
    count = lax.axis_size(axis)
    return (
        lax.ppermute(block, axis, [(i, (i + 1) % count) for i in range(count)]),
        lax.ppermute(block, axis, [((i + 1) % count, i) for i in range(count)]),
    )


def per_device(start, probe, offsets, orbitals, index, kinds, hop_table, onsite_table):
    vectors = start.shape[1]
    slots = offsets.shape[0]
    width = 2
    cells = 2 * vectors * TILES
    edge_tiles = vectors + (KINDS + 3) // 4
    wide_tiles = cells + KINDS + (KINDS + 1) // 2
    table = jnp.pad(hop_table, (0, LANES - hop_table.shape[0]))[None]
    levels = jnp.pad(onsite_table, (0, LANES - onsite_table.shape[0]))[None]
    block = (ROWS, LANES)
    coef, to_right, to_left = call(
        functools.partial(pack_kernel, vectors, slots),
        [(KINDS, *block), (edge_tiles, *block), (edge_tiles, *block)],
    )(start, offsets, index, kinds, table, levels)
    count = lax.axis_size("gy")
    from_left = lax.ppermute(to_right, "gy", [(i, (i + 1) % count) for i in range(count)])
    from_right = lax.ppermute(to_left, "gy", [((i + 1) % count, i) for i in range(count)])
    (wide,) = call(functools.partial(widen_kernel, vectors), [(wide_tiles, *block)])(
        start, coef, from_left, from_right
    )
    scratch = [(cells, REGION, LANES)] * APPLY + [(2 * vectors, *block)]
    below, above = neighbours(wide, "gx")
    state, coefs, first = call(
        functools.partial(first_kernel, vectors, width),
        [(cells, *block), (COEF_ROWS * TILES, REGION, LANES), (1, LANES)],
        scratch,
    )(wide, below, above, probe)
    sums = [first]
    for _ in range(STEPS - 2):
        below, above = neighbours(state, "gx")
        state, part = call(
            functools.partial(middle_kernel, vectors, width), [(cells, *block), (1, LANES)], scratch
        )(state, below, above, coefs, probe)
        sums.append(part)
    below, above = neighbours(state, "gx")
    final, rows = call(
        functools.partial(last_kernel, vectors, width),
        [start.shape, (lax.axis_size("gx"), STEPS, LANES)],
        scratch,
    )(state, below, above, coefs, probe, *sums)
    part = jnp.sum(lax.all_to_all(rows, "gx", 0, 0), axis=0)
    copies = jnp.broadcast_to(part[None], (count, STEPS, LANES))
    total = jnp.sum(lax.all_to_all(copies, "gy", 0, 0), axis=0)
    total_cells = start.shape[3] * start.shape[4] * lax.axis_size("gx") * count
    norm = 1.0 / math.sqrt(2.0 * 2 * total_cells)
    return final, total[:, : 2 * vectors].reshape(STEPS, 2, vectors) * norm


def solution(mesh):
    return jax.shard_map(
        per_device,
        mesh=mesh,
        in_specs=(
            P(None, None, None, "gx", "gy"),
            P(None, None, None, "gx", "gy"),
            P(None, None, "gx", "gy"),
            P(None, None, "gx", "gy"),
            P(None, None, "gx", "gy"),
            P(None, "gx", "gy"),
            P(),
            P(),
        ),
        out_specs=(P(None, None, None, "gx", "gy"), P()),
        check_vma=False,
    )
```

```python
import functools
import math

import jax
import jax.numpy as jnp
from jax import lax
from jax.experimental import pallas as pl
from jax.experimental.pallas import tpu as pltpu
from jax.sharding import PartitionSpec as P

APPLY = 4
STEPS = 4
TIME_STEP = 2.6

ROWS = 8
LANES = 128
EDGE = 32
REGION = 3 * ROWS
TILES = 3
PARTS = 2
VMEM_LIMIT = 48 * 1024 * 1024

HALF = [(p, q) for p in range(3) for q in range(-2, 3) if p > 0 or q > 0]
CROSS = 2 * len(HALF)
ONSITE = CROSS + 1
KINDS = ONSITE + 2
SHIFTED = [(number, half) for number, half in enumerate(HALF) if half[1] != 0]
SHIFT_SLOT = {half: 2 * place for place, (_, half) in enumerate(SHIFTED)}
COEF_ROWS = KINDS + 2 * len(SHIFTED)


def bessel(order, arg):
    total = 0.0
    for term in range(40):
        total += (
            (-1.0) ** term
            * (arg / 2.0) ** (2 * term + order)
            / (math.factorial(term) * math.factorial(term + order))
        )
    return total


def roll(tile, amount):
    amount = amount % LANES
    return tile if amount == 0 else pltpu.roll(tile, amount, 1)


def lane_ids():
    return lax.broadcasted_iota(jnp.int32, (ROWS, LANES), 1)


def shift_tiles(tiles, amount, lanes):
    even, odd, tail = (roll(tile, amount) for tile in tiles)
    if amount > 0:
        tail = jnp.where(lanes < amount, even, tail)
        tail = jnp.where((lanes >= 64) & (lanes < 64 + amount), odd, tail)
    else:
        even = jnp.where(lanes >= LANES + amount, tail, even)
        odd = jnp.where((lanes >= 64 + amount) & (lanes < 64), tail, odd)
    return even, odd, tail


def in_group(lanes, group):
    return (lanes >= EDGE * group) & (lanes < EDGE * (group + 1))


def turned(real, imag):
    return roll(real, EDGE), roll(imag, EDGE + 64)


def fetch(pairs, semaphores):
    copies = [pltpu.make_async_copy(source, target, semaphores.at[i]) for i, (source, target) in enumerate(pairs)]
    for copy in copies:
        copy.start()
    for copy in copies:
        copy.wait()


def pack_kernel(
    vectors, slots, start, probe, offsets, index, kinds, hop_table, onsite_table, parities,
    probe_copy, block, pair_one, pair_two, state, offsets_here, index_here, kinds_here, table_here, semaphores,
):
    fetch(
        [
            (start, state), (offsets, offsets_here), (index, index_here), (kinds, kinds_here),
            (hop_table, table_here), (probe, probe_copy),
        ],
        semaphores,
    )
    lanes = lane_ids()
    even = jnp.full((ROWS, LANES), parities[1], jnp.int32) == 0
    coefs_at = 4 * vectors

    def send(at, to_right, to_left):
        pair_one[at] = jnp.where(even, to_right, to_left)
        pair_two[at] = jnp.where(even, to_left, to_right)

    low = lanes < 64
    first = in_group(lanes, 0) | in_group(lanes, 2)
    for v in range(vectors):
        strips = []
        for a in range(2):
            block[4 * v + 2 * a] = state[0, v, a]
            block[4 * v + 2 * a + 1] = state[1, v, a]
            real, imag = turned(state[0, v, a], state[1, v, a])
            strips.append(jnp.where(low, real, imag))
        to_right = jnp.where(first, strips[0], roll(strips[1], EDGE))
        to_left = jnp.where(first, roll(strips[1], -EDGE), strips[0])
        send(v, to_right, to_left)
    entries = table_here[...]
    spare = LANES - entries.shape[1]
    table = jnp.broadcast_to(jnp.concatenate([entries, jnp.zeros((1, spare), jnp.float32)], axis=1), (ROWS, LANES))
    arrays = [jnp.zeros((ROWS, LANES), jnp.float32) for _ in range(KINDS)]
    for a in range(2):
        for slot in range(slots):
            amount = jnp.take_along_axis(table, index_here[slot, a], axis=1)
            code = offsets_here[slot, a]
            for number, (p, q) in enumerate(HALF):
                at = 2 * number + a
                arrays[at] = arrays[at] + jnp.where(code == 5 * (p + 2) + q + 2, amount, 0.0)
            if a == 0:
                arrays[CROSS] = arrays[CROSS] + jnp.where(code == 12, amount, 0.0)
        for entry in range(onsite_table.shape[0]):
            arrays[ONSITE + a] = jnp.where(kinds_here[a] == entry, onsite_table[entry], arrays[ONSITE + a])
    for start_at in range(0, KINDS, 4):
        right = left = None
        for group in range(min(4, KINDS - start_at)):
            double = 2.0 * arrays[start_at + group]
            block[coefs_at + start_at + group] = double
            base = roll(double, EDGE)
            from_tail = roll(base, EDGE * group)
            from_head = roll(base, EDGE * (group - 1))
            right = from_tail if right is None else jnp.where(in_group(lanes, group), from_tail, right)
            left = from_head if left is None else jnp.where(in_group(lanes, group), from_head, left)
        send(vectors + start_at // 4, right, left)


def sides(strips, parity):
    edge = strips.shape[0] // 2
    left_at = jnp.where(parity == 0, edge, 0)
    return lambda at: strips[left_at + at], lambda at: strips[edge - left_at + at]


def widen_state(block, left_of, right_of, v, a, lanes):
    real, imag = turned(block[4 * v + 2 * a], block[4 * v + 2 * a + 1])
    left = roll(left_of(v), -EDGE * a)
    right = roll(right_of(v), EDGE * a)
    first, third = in_group(lanes, 0), in_group(lanes, 2)
    return (
        jnp.where(first, left, real),
        jnp.where(third, left, imag),
        jnp.where(first, real, jnp.where(third, imag, right)),
    )


def widen_coef(vectors, block, left_of, right_of, j, lanes):
    group = j % 4
    body = roll(block[4 * vectors + j], EDGE)
    left = roll(left_of(vectors + j // 4), -EDGE * group)
    right = roll(right_of(vectors + j // 4), EDGE * (1 - group))
    first = in_group(lanes, 0)
    even = jnp.where(first, left, body)
    tail = jnp.where(first, body, right)
    return even, roll(even, 64), jnp.where(lanes < 64, tail, roll(tail, 64))


def spread(vectors, block, left_of, right_of, put):
    lanes = lane_ids()
    for j in range(KINDS):
        tiles = widen_coef(vectors, block, left_of, right_of, j, lanes)
        for t in range(TILES):
            put(TILES * j + t, tiles[t])
        if j < CROSS and HALF[j // 2][1] != 0:
            moved = shift_tiles(tiles, HALF[j // 2][1], lanes)
            at = KINDS + SHIFT_SLOT[HALF[j // 2]] + j % 2
            for t in range(TILES):
                put(TILES * at + t, moved[t])


def own_kernel(vectors, block, strips, parities, wide, coefs):
    lanes = lane_ids()
    left_of, right_of = sides(strips, parities[1])
    for v in range(vectors):
        for a in range(2):
            tiles = widen_state(block, left_of, right_of, v, a, lanes)
            for t in range(TILES):
                wide[(2 * v + a) * TILES + t] = tiles[t]

    def put(at, tile):
        coefs[at] = tile

    spread(vectors, block, left_of, right_of, put)


def pair_tops(parities):
    last = 2 * ROWS
    top = pl.multiple_of(jnp.where(parities[0] == 0, last, 0), ROWS)
    return top, pl.multiple_of(last - top, ROWS)


def coefficient(coefs, dx, dy, a, t, top):
    source = a if (dx + dy) % 2 else 1 - a
    if (dx, dy) == (0, 0):
        at, row = CROSS, top
    elif (dx, dy) in HALF:
        at = KINDS + SHIFT_SLOT[(dx, dy)] + a if dy else 2 * HALF.index((dx, dy)) + a
        row = top
    else:
        at, row = 2 * HALF.index((-dx, -dy)) + source, top + dx
    return source, coefs[TILES * at + t, pl.ds(row, ROWS), :]


def apply_twice(field, coefs, a, group, width, top, lanes):
    sums = [[[None] * 5 for _ in range(TILES)] for _ in range(width)]
    for dx in range(-2, 3):
        rows = pl.ds(top + dx, ROWS)
        for t in range(TILES):
            values = [
                [field[((group * width + w) * 2 + b) * TILES + t, rows, :] for b in range(2)]
                for w in range(width)
            ]
            for dy in range(-2, 3):
                source, factor = coefficient(coefs, dx, dy, a, t, top)
                for w in range(width):
                    term = factor * values[w][source]
                    old = sums[w][t][dy + 2]
                    sums[w][t][dy + 2] = term if old is None else old + term
            if dx == 0:
                factor = coefs[TILES * (ONSITE + a) + t, pl.ds(top, ROWS), :]
                for w in range(width):
                    sums[w][t][2] = sums[w][t][2] + factor * values[w][a]
    results = []
    for w in range(width):
        total = [sums[w][t][2] for t in range(TILES)]
        for dy in (-2, -1, 1, 2):
            moved = shift_tiles([sums[w][t][dy + 2] for t in range(TILES)], -dy, lanes)
            total = [total[t] + moved[t] for t in range(TILES)]
        results.append(total)
    return results


def time_step(half, width, coefs, probe, terms, products, finish):
    vectors, start = half
    lanes = lane_ids()
    scale = [bessel(order, TIME_STEP) * (1.0 if order == 0 else 2.0) for order in range(APPLY + 1)]
    for order in range(1, APPLY + 1):
        low, high = 2 * order, REGION - 2 * order
        tops = list(range(low, high - ROWS + 1, ROWS))
        if tops[-1] != high - ROWS:
            tops.append(high - ROWS)
        for a in range(2):

            def body(group, carry):
                for top in tops:
                    images = apply_twice(terms[order - 1], coefs, a, group, width, top, lanes)
                    for w in range(width):
                        v = group * width + w
                        at = (2 * v + a) * TILES
                        rows = pl.ds(top, ROWS)
                        if order == 1:
                            new = [0.5 * images[w][t] for t in range(TILES)]
                        else:
                            new = [images[w][t] - terms[order - 2][at + t, rows, :] for t in range(TILES)]
                        if order < APPLY:
                            for t in range(TILES):
                                terms[order][at + t, rows, :] = new[t]
                            continue
                        even = []
                        odd = []
                        for t in range(TILES):
                            part = [terms[k][at + t, rows, :] for k in range(APPLY)]
                            even.append(scale[0] * part[0] - scale[2] * part[2] + scale[4] * new[t])
                            odd.append(roll(scale[1] * part[1] - scale[3] * part[3], 64))
                        real = even[0] + odd[1]
                        imag = even[1] - odd[0]
                        tail = even[2] + jnp.where(lanes < 64, odd[2], -odd[2])
                        own_real = roll(jnp.where(in_group(lanes, 0), tail, real), -EDGE)
                        own_imag = roll(jnp.where(in_group(lanes, 2), tail, imag), -EDGE - 64)
                        probe_real, probe_imag = probe[0, start + v, a], probe[1, start + v, a]
                        same = probe_real * own_real + probe_imag * own_imag
                        cross = probe_real * own_imag - probe_imag * own_real
                        if a == 1:
                            same = same + products[v]
                            cross = cross + products[vectors + v]
                        products[v] = same
                        products[vectors + v] = cross
                        finish(at, v, a, (real, imag, tail), (own_real, own_imag))
                return carry

            lax.fori_loop(0, vectors // width, body, 0)


def probe_row(half, whole, products):
    vectors, start = half
    sums = jnp.sum(jnp.sum(products[...], axis=1), axis=1, keepdims=True)
    rows = lax.broadcasted_iota(jnp.int32, (2 * vectors, LANES), 0)
    lanes = lax.broadcasted_iota(jnp.int32, (2 * vectors, LANES), 1)
    place = jnp.where(rows < vectors, start + rows, whole + start + rows - vectors)
    return jnp.sum(jnp.where(lanes == place, sums, 0.0), axis=0, keepdims=True)


def add_row(half, whole, step, rows, products):
    here = lax.broadcasted_iota(jnp.int32, (STEPS, LANES), 0) == step
    row = jnp.where(here, probe_row(half, whole, products), 0.0)
    return row if rows is None else rows[...] + row


def put_state(state):
    def finish(at, v, a, tiles, cells):
        for t in range(TILES):
            state[at + t] = tiles[t]

    return finish


def put_cells(state, start):
    def finish(at, v, a, tiles, cells):
        state[0, start + v, a] = cells[0]
        state[1, start + v, a] = cells[1]

    return finish


def first_kernel(
    half, whole, width, wide, coefs_own, block_one, block_two, strips_one, strips_two, probe, parities, *refs
):
    lanes = lane_ids()
    vectors, _ = half
    split = vectors < whole
    state, coefs = refs[:2]
    other, rows = refs[2:4] if split else (None, refs[2])
    t0, t1, t2, t3, products = refs[-5:]
    for at in range(2 * whole * TILES):
        into, place = (t0, at) if at < t0.shape[0] else (other, at - t0.shape[0])
        into[place, pl.ds(ROWS, ROWS), :] = wide[at]
    for at in range(COEF_ROWS * TILES):
        coefs[at, pl.ds(ROWS, ROWS), :] = coefs_own[at]
    for top, block, strips in zip(pair_tops(parities), (block_one, block_two), (strips_one, strips_two)):
        left_of, right_of = sides(strips, parities[1])
        for v in range(whole):
            for a in range(2):
                tiles = widen_state(block, left_of, right_of, v, a, lanes)
                for t in range(TILES):
                    into = t0 if v < vectors else other
                    into[(2 * (v % vectors) + a) * TILES + t, pl.ds(top, ROWS), :] = tiles[t]

        def put(at, tile, top=top):
            coefs[at, pl.ds(top, ROWS), :] = tile

        spread(whole, block, left_of, right_of, put)
    time_step(half, width, coefs, probe, (t0, t1, t2, t3), products, put_state(state))
    rows[...] = add_row(half, whole, 0, None, products)


def second_kernel(half, whole, width, t0, coefs, probe, rows_in, state, rows, t1, t2, t3, products):
    time_step(half, width, coefs, probe, (t0, t1, t2, t3), products, put_state(state))
    rows[...] = add_row(half, whole, 0, rows_in, products)


def gather_rows(first, own, one, two, parities):
    top_one, top_two = pair_tops(parities)
    for top, block in ((ROWS, own), (top_one, one), (top_two, two)):
        for at in range(first.shape[0]):
            first[at, pl.ds(top, ROWS), :] = block[at]


def middle_kernel(
    half, whole, width, step, own, one, two, coefs, probe, parities, rows_in, state, rows, t0, t1, t2, t3, products
):
    gather_rows(t0, own, one, two, parities)
    time_step(half, width, coefs, probe, (t0, t1, t2, t3), products, put_state(state))
    rows[...] = add_row(half, whole, step, rows_in, products)


def close_kernel(half, whole, width, own, one, two, coefs, probe, parities, rows_in, state, rows, t0, t1, t2, t3, products):
    gather_rows(t0, own, one, two, parities)
    time_step(half, width, coefs, probe, (t0, t1, t2, t3), products, put_cells(state, 0))
    rows[...] = add_row(half, whole, STEPS - 1, rows_in, products)


def last_kernel(half, whole, width, own, one, two, coefs, probe, parities, rows_in, *refs):
    state, copies, t0, t1, t2, t3, products = refs[-7:]
    gather_rows(t0, own, one, two, parities)
    for done in refs[:-7]:
        for part in range(2):
            for v in range(done.shape[1]):
                for a in range(2):
                    state[part, v, a] = done[part, v, a]
    time_step(half, width, coefs, probe, (t0, t1, t2, t3), products, put_cells(state, half[1]))
    rows = add_row(half, whole, STEPS - 1, rows_in, products)
    for copy in range(copies.shape[0]):
        copies[copy] = rows


def call(kernel, out_shapes, scratch=(), scalars=None, operands=0):
    in_memory = pl.BlockSpec(memory_space=pltpu.VMEM)
    specs = [pl.BlockSpec(memory_space=pltpu.SMEM) if i == scalars else in_memory for i in range(operands)]
    return pl.pallas_call(
        kernel,
        out_shape=[jax.ShapeDtypeStruct(shape, jnp.float32) for shape in out_shapes],
        in_specs=specs,
        scratch_shapes=[pltpu.VMEM(shape, jnp.float32) for shape in scratch],
        compiler_params=pltpu.CompilerParams(vmem_limit_bytes=VMEM_LIMIT),
    )


def pairings(axis):
    count = lax.axis_size(axis)
    one = [(i, i + 1 - 2 * (i % 2)) for i in range(count)]
    two = [(i, (i - 1 + 2 * (i % 2)) % count) for i in range(count)]
    return one, two


def swap(block, axis):
    one, two = pairings(axis)
    return lax.ppermute(block, axis, one), lax.ppermute(block, axis, two)


def sum_kernel(vectors, norm, rows, result):
    total = rows[0]
    for i in range(1, rows.shape[0]):
        total = total + rows[i]
    total = total * norm
    result[:, 0, :] = total[:, :vectors]
    result[:, 1, :] = total[:, vectors : 2 * vectors]


def per_device(start, probe, offsets, orbitals, index, kinds, hop_table, onsite_table):
    whole = start.shape[1]
    slots = offsets.shape[0]
    vectors = whole // PARTS
    width = 4
    groups = [(vectors, vectors * g) for g in range(PARTS)]
    cells = 2 * vectors * TILES
    edge_tiles = whole + (KINDS + 3) // 4
    tile = (ROWS, LANES)
    rows_shape = (STEPS, LANES)
    region = (cells, REGION, LANES)
    scratch = [region] * APPLY + [(2 * vectors, *tile)]
    parities = jnp.stack([lax.axis_index("gx") % 2, lax.axis_index("gy") % 2]).astype(jnp.int32)

    in_hbm = pl.BlockSpec(memory_space=pltpu.HBM)
    in_smem = pl.BlockSpec(memory_space=pltpu.SMEM)
    probe, block, pair_one, pair_two = pl.pallas_call(
        functools.partial(pack_kernel, whole, slots),
        out_shape=[
            jax.ShapeDtypeStruct(shape, jnp.float32)
            for shape in (probe.shape, (4 * whole + KINDS, *tile), (edge_tiles, *tile), (edge_tiles, *tile))
        ],
        in_specs=[in_hbm] * 6 + [in_smem] * 2,
        scratch_shapes=[
            pltpu.VMEM(start.shape, jnp.float32),
            pltpu.VMEM(offsets.shape, jnp.int32),
            pltpu.VMEM(index.shape, jnp.int32),
            pltpu.VMEM(kinds.shape, jnp.int32),
            pltpu.VMEM((1, hop_table.shape[0]), jnp.float32),
            pltpu.SemaphoreType.DMA((6,)),
        ],
        compiler_params=pltpu.CompilerParams(vmem_limit_bytes=VMEM_LIMIT),
    )(start, probe, offsets, index, kinds, hop_table[None], onsite_table, parities)
    one, two = pairings("gy")
    strips = jnp.concatenate([lax.ppermute(pair_one, "gy", one), lax.ppermute(pair_two, "gy", two)])
    block_one, block_two = swap(block, "gx")
    strips_one, strips_two = swap(strips, "gx")
    wide, coefs_own = call(
        functools.partial(own_kernel, whole),
        [(2 * whole * TILES, *tile), (COEF_ROWS * TILES, *tile)],
        scalars=2,
        operands=3,
    )(block, strips, parities)

    state_shape = (cells, *tile)
    others = [region] * (PARTS - 1)
    first, coefs, *others, rows = call(
        functools.partial(first_kernel, groups[0], whole, width),
        [state_shape, (COEF_ROWS * TILES, REGION, LANES), *others, rows_shape],
        scratch,
        scalars=7,
        operands=8,
    )(wide, coefs_own, block_one, block_two, strips_one, strips_two, probe, parities)
    states = [first]
    for g, other in enumerate(others, 1):
        state, rows = call(
            functools.partial(second_kernel, groups[g], whole, width), [state_shape, rows_shape], scratch[1:], operands=4
        )(other, coefs, probe, rows)
        states.append(state)
    for step in range(1, STEPS - 1):
        for g in range(PARTS):
            states[g], rows = call(
                functools.partial(middle_kernel, groups[g], whole, width, step),
                [state_shape, rows_shape],
                scratch,
                scalars=5,
                operands=7,
            )(states[g], *swap(states[g], "gx"), coefs, probe, parities, rows)
    done = []
    for g in range(PARTS - 1):
        state, rows = call(
            functools.partial(close_kernel, groups[g], whole, width),
            [(2, vectors, *start.shape[2:]), rows_shape],
            scratch,
            scalars=5,
            operands=7,
        )(states[g], *swap(states[g], "gx"), coefs, probe, parities, rows)
        done.append(state)
    final, copies = call(
        functools.partial(last_kernel, groups[-1], whole, width),
        [start.shape, (lax.axis_size("gx"), *rows_shape)],
        scratch,
        scalars=5,
        operands=7 + len(done),
    )(states[-1], *swap(states[-1], "gx"), coefs, probe, parities, rows, *done)
    part = jnp.sum(lax.all_to_all(copies, "gx", 0, 0), axis=0)
    count = lax.axis_size("gy")
    copies = jnp.broadcast_to(part[None], (count, *rows_shape))
    total_cells = start.shape[3] * start.shape[4] * lax.axis_size("gx") * count
    norm = 1.0 / math.sqrt(2.0 * 2 * total_cells)
    (intersections,) = call(functools.partial(sum_kernel, whole, norm), [(STEPS, 2, whole)], operands=1)(
        lax.all_to_all(copies, "gy", 0, 0)
    )
    return final, intersections


def solution(mesh):
    return jax.shard_map(
        per_device,
        mesh=mesh,
        in_specs=(
            P(None, None, None, "gx", "gy"),
            P(None, None, None, "gx", "gy"),
            P(None, None, "gx", "gy"),
            P(None, None, "gx", "gy"),
            P(None, None, "gx", "gy"),
            P(None, "gx", "gy"),
            P(),
            P(),
        ),
        out_specs=(P(None, None, None, "gx", "gy"), P()),
        check_vma=False,
    )
```

```python
import functools
import math

import jax
import jax.numpy as jnp
from jax import lax
from jax.experimental import pallas as pl
from jax.experimental.pallas import tpu as pltpu
from jax.sharding import PartitionSpec as P

APPLY = 4
STEPS = 4
TIME_STEP = 2.6

ROWS = 8
LANES = 128
EDGE = 32
REGION = 3 * ROWS
TILES = 3
PARTS = 2
VMEM_LIMIT = 48 * 1024 * 1024

HALF = [(p, q) for p in range(3) for q in range(-2, 3) if p > 0 or q > 0]
CROSS = 2 * len(HALF)
ONSITE = CROSS + 1
KINDS = ONSITE + 2
SHIFTED = [(number, half) for number, half in enumerate(HALF) if half[1] != 0]
SHIFT_SLOT = {half: 2 * place for place, (_, half) in enumerate(SHIFTED)}
COEF_ROWS = KINDS + 2 * len(SHIFTED)


def bessel(order, arg):
    total = 0.0
    for term in range(40):
        total += (
            (-1.0) ** term
            * (arg / 2.0) ** (2 * term + order)
            / (math.factorial(term) * math.factorial(term + order))
        )
    return total


def roll(tile, amount):
    amount = amount % LANES
    return tile if amount == 0 else pltpu.roll(tile, amount, 1)


def lane_ids():
    return lax.broadcasted_iota(jnp.int32, (ROWS, LANES), 1)


def shift_tiles(tiles, amount, lanes):
    even, odd, tail = (roll(tile, amount) for tile in tiles)
    if amount > 0:
        tail = jnp.where(lanes < amount, even, tail)
        tail = jnp.where((lanes >= 64) & (lanes < 64 + amount), odd, tail)
    else:
        even = jnp.where(lanes >= LANES + amount, tail, even)
        odd = jnp.where((lanes >= 64 + amount) & (lanes < 64), tail, odd)
    return even, odd, tail


def in_batches(size, jobs):
    jobs = list(jobs)
    for start in range(0, len(jobs), size):
        triples = [triple for job in jobs[start : start + size] for triple in job()]
        for store, place, value in triples:
            store(place, value)


def into(ref, rows=None):
    def store(place, value):
        if rows is None:
            ref[place] = value
        else:
            ref[place, pl.ds(rows, ROWS), :] = value

    return store


def copies(store, read, count, shift=0):
    return [lambda at=at: [(store, at, read(at + shift))] for at in range(count)]


def in_group(lanes, group):
    return (lanes >= EDGE * group) & (lanes < EDGE * (group + 1))


def turned(real, imag):
    return roll(real, EDGE), roll(imag, EDGE + 64)


def fetch(pairs, semaphores):
    copies = [pltpu.make_async_copy(source, target, semaphores.at[i]) for i, (source, target) in enumerate(pairs)]
    for copy in copies:
        copy.start()
    for copy in copies:
        copy.wait()


def pack_kernel(
    vectors, slots, start, probe, offsets, index, kinds, hop_table, onsite_table, parities,
    probe_copy, state, coef, pair_one, pair_two, offsets_here, index_here, kinds_here, table_here, semaphores,
):
    fetch(
        [
            (start, state), (offsets, offsets_here), (index, index_here), (kinds, kinds_here),
            (hop_table, table_here), (probe, probe_copy),
        ],
        semaphores,
    )
    lanes = lane_ids()
    even = is_even(parities[1])

    def send(at, to_right, to_left):
        return [
            (into(pair_one), at, jnp.where(even, to_right, to_left)),
            (into(pair_two), at, jnp.where(even, to_left, to_right)),
        ]

    low = lanes < 64
    first = in_group(lanes, 0) | in_group(lanes, 2)

    def strip(v):
        strips = []
        for a in range(2):
            real, imag = turned(state[0, v, a], state[1, v, a])
            strips.append(jnp.where(low, real, imag))
        to_right = jnp.where(first, strips[0], roll(strips[1], EDGE))
        to_left = jnp.where(first, roll(strips[1], -EDGE), strips[0])
        return send(v, to_right, to_left)

    in_batches(vectors, [functools.partial(strip, v) for v in range(vectors)])
    entries = table_here[...]
    spare = LANES - entries.shape[1]
    table = jnp.broadcast_to(jnp.concatenate([entries, jnp.zeros((1, spare), jnp.float32)], axis=1), (ROWS, LANES))
    arrays = [jnp.zeros((ROWS, LANES), jnp.float32) for _ in range(KINDS)]
    for a in range(2):
        for slot in range(slots):
            amount = jnp.take_along_axis(table, index_here[slot, a], axis=1)
            code = offsets_here[slot, a]
            for number, (p, q) in enumerate(HALF):
                at = 2 * number + a
                arrays[at] = arrays[at] + jnp.where(code == 5 * (p + 2) + q + 2, amount, 0.0)
            if a == 0:
                arrays[CROSS] = arrays[CROSS] + jnp.where(code == 12, amount, 0.0)
        for entry in range(onsite_table.shape[0]):
            arrays[ONSITE + a] = jnp.where(kinds_here[a] == entry, onsite_table[entry], arrays[ONSITE + a])
    for start_at in range(0, KINDS, 4):
        right = left = None
        for group in range(min(4, KINDS - start_at)):
            double = 2.0 * arrays[start_at + group]
            coef[start_at + group] = double
            base = roll(double, EDGE)
            from_tail = roll(base, EDGE * group)
            from_head = roll(base, EDGE * (group - 1))
            right = from_tail if right is None else jnp.where(in_group(lanes, group), from_tail, right)
            left = from_head if left is None else jnp.where(in_group(lanes, group), from_head, left)
        for store, place, value in send(vectors + start_at // 4, right, left):
            store(place, value)


def is_even(parity):
    return jnp.full((ROWS, LANES), parity, jnp.int32) == 0


def ordered(one, two, even):
    return (
        lambda at: jnp.where(even, two[at], one[at]),
        lambda at: jnp.where(even, one[at], two[at]),
    )


def halves(strips):
    edge = strips.shape[0] // 2
    return strips.at[pl.ds(0, edge)], strips.at[pl.ds(edge, edge)]


def widen_state(read, left_of, right_of, v, a, lanes):
    real, imag = turned(read(4 * v + 2 * a), read(4 * v + 2 * a + 1))
    left = roll(left_of(v), -EDGE * a)
    right = roll(right_of(v), EDGE * a)
    first, third = in_group(lanes, 0), in_group(lanes, 2)
    return (
        jnp.where(first, left, real),
        jnp.where(third, left, imag),
        jnp.where(first, real, jnp.where(third, imag, right)),
    )


def widen_coef(vectors, read, left_of, right_of, j, lanes):
    group = j % 4
    body = roll(read(4 * vectors + j), EDGE)
    left = roll(left_of(vectors + j // 4), -EDGE * group)
    right = roll(right_of(vectors + j // 4), EDGE * (1 - group))
    first = in_group(lanes, 0)
    even = jnp.where(first, left, body)
    tail = jnp.where(first, body, right)
    return even, roll(even, 64), jnp.where(lanes < 64, tail, roll(tail, 64))


def spread(vectors, read, left_of, right_of, store):
    lanes = lane_ids()

    def job(j):
        tiles = widen_coef(vectors, read, left_of, right_of, j, lanes)
        result = [(store, TILES * j + t, tiles[t]) for t in range(TILES)]
        if j < CROSS and HALF[j // 2][1] != 0:
            moved = shift_tiles(tiles, HALF[j // 2][1], lanes)
            at = KINDS + SHIFT_SLOT[HALF[j // 2]] + j % 2
            result += [(store, TILES * at + t, moved[t]) for t in range(TILES)]
        return result

    in_batches(4, [functools.partial(job, j) for j in range(KINDS)])


def spread_state(vectors, read, left_of, right_of, store_of):
    lanes = lane_ids()

    def job(v, a):
        store, place = store_of(v, a)
        tiles = widen_state(read, left_of, right_of, v, a, lanes)
        return [(store, place + t, tiles[t]) for t in range(TILES)]

    in_batches(4, [functools.partial(job, v, a) for v in range(vectors) for a in range(2)])


def block_kernel(vectors, state, coef, block):
    in_batches(
        16, [lambda v=v, a=a, c=c: [(into(block), 4 * v + 2 * a + c, state[c, v, a])] for v in range(vectors) for a in range(2) for c in range(2)]
    )
    in_batches(16, [lambda j=j: [(into(block), 4 * vectors + j, coef[j])] for j in range(KINDS)])


def own_kernel(vectors, block, strips, parities, wide, coefs):
    left_of, right_of = ordered(*halves(strips), is_even(parities[1]))
    read = lambda at: block[at]
    spread_state(vectors, read, left_of, right_of, lambda v, a: (into(wide), (2 * v + a) * TILES))
    spread(vectors, read, left_of, right_of, into(coefs))


def coefficient(coefs, dx, dy, a, t, top):
    source = a if (dx + dy) % 2 else 1 - a
    if (dx, dy) == (0, 0):
        at, row = CROSS, top
    elif (dx, dy) in HALF:
        at = KINDS + SHIFT_SLOT[(dx, dy)] + a if dy else 2 * HALF.index((dx, dy)) + a
        row = top
    else:
        at, row = 2 * HALF.index((-dx, -dy)) + source, top + dx
    return source, coefs[TILES * at + t, pl.ds(row, ROWS), :]


def apply_twice(field, coefs, a, group, width, top, lanes):
    sums = [[[None] * 5 for _ in range(TILES)] for _ in range(width)]
    for dx in range(-2, 3):
        rows = pl.ds(top + dx, ROWS)
        for t in range(TILES):
            values = [
                [field[((group * width + w) * 2 + b) * TILES + t, rows, :] for b in range(2)]
                for w in range(width)
            ]
            for dy in range(-2, 3):
                source, factor = coefficient(coefs, dx, dy, a, t, top)
                for w in range(width):
                    term = factor * values[w][source]
                    old = sums[w][t][dy + 2]
                    sums[w][t][dy + 2] = term if old is None else old + term
            if dx == 0:
                factor = coefs[TILES * (ONSITE + a) + t, pl.ds(top, ROWS), :]
                for w in range(width):
                    sums[w][t][2] = sums[w][t][2] + factor * values[w][a]
    results = []
    for w in range(width):
        total = [sums[w][t][2] for t in range(TILES)]
        for dy in (-2, -1, 1, 2):
            moved = shift_tiles([sums[w][t][dy + 2] for t in range(TILES)], -dy, lanes)
            total = [total[t] + moved[t] for t in range(TILES)]
        results.append(total)
    return results


def time_step(half, width, coefs, probe, terms, products, finish):
    vectors, start = half
    lanes = lane_ids()
    scale = [bessel(order, TIME_STEP) * (1.0 if order == 0 else 2.0) for order in range(APPLY + 1)]
    for order in range(1, APPLY + 1):
        low, high = 2 * order, REGION - 2 * order
        tops = list(range(low, high - ROWS + 1, ROWS))
        if tops[-1] != high - ROWS:
            tops.append(high - ROWS)
        for a in range(2):

            def body(group, carry):
                for top in tops:
                    images = apply_twice(terms[order - 1], coefs, a, group, width, top, lanes)
                    stores = []
                    for w in range(width):
                        v = group * width + w
                        at = (2 * v + a) * TILES
                        rows = pl.ds(top, ROWS)
                        if order == 1:
                            new = [0.5 * images[w][t] for t in range(TILES)]
                        else:
                            new = [images[w][t] - terms[order - 2][at + t, rows, :] for t in range(TILES)]
                        if order < APPLY:
                            stores += [(into(terms[order], top), at + t, new[t]) for t in range(TILES)]
                            continue
                        even = []
                        odd = []
                        for t in range(TILES):
                            part = [terms[k][at + t, rows, :] for k in range(APPLY)]
                            even.append(scale[0] * part[0] - scale[2] * part[2] + scale[4] * new[t])
                            odd.append(roll(scale[1] * part[1] - scale[3] * part[3], 64))
                        real = even[0] + odd[1]
                        imag = even[1] - odd[0]
                        tail = even[2] + jnp.where(lanes < 64, odd[2], -odd[2])
                        own_real = roll(jnp.where(in_group(lanes, 0), tail, real), -EDGE)
                        own_imag = roll(jnp.where(in_group(lanes, 2), tail, imag), -EDGE - 64)
                        probe_real, probe_imag = probe[0, start + v, a], probe[1, start + v, a]
                        same = probe_real * own_real + probe_imag * own_imag
                        cross = probe_real * own_imag - probe_imag * own_real
                        if a == 1:
                            same = same + products[v]
                            cross = cross + products[vectors + v]
                        stores += [(into(products), v, same), (into(products), vectors + v, cross)]
                        stores += finish(at, v, a, (real, imag, tail), (own_real, own_imag))
                    for store, place, value in stores:
                        store(place, value)
                return carry

            lax.fori_loop(0, vectors // width, body, 0)


def probe_row(half, whole, products):
    vectors, start = half
    sums = jnp.sum(jnp.sum(products[...], axis=1), axis=1, keepdims=True)
    rows = lax.broadcasted_iota(jnp.int32, (2 * vectors, LANES), 0)
    lanes = lax.broadcasted_iota(jnp.int32, (2 * vectors, LANES), 1)
    place = jnp.where(rows < vectors, start + rows, whole + start + rows - vectors)
    return jnp.sum(jnp.where(lanes == place, sums, 0.0), axis=0, keepdims=True)


def add_row(half, whole, step, rows, products):
    here = lax.broadcasted_iota(jnp.int32, (STEPS, LANES), 0) == step
    row = jnp.where(here, probe_row(half, whole, products), 0.0)
    return row if rows is None else rows[...] + row


def put_state(state):
    return lambda at, v, a, tiles, cells: [(into(state), at + t, tiles[t]) for t in range(TILES)]


def put_cells(state, start):
    return lambda at, v, a, tiles, cells: [(into(state), (c, start + v, a), cells[c]) for c in range(2)]


def first_kernel(
    half, whole, width, wide, coefs_own, block_one, block_two, strips_one, strips_two, probe, parities, *refs
):
    vectors, _ = half
    split = vectors < whole
    state, coefs = refs[:2]
    other, rows = refs[2:4] if split else (None, refs[2])
    t0, t1, t2, t3, products = refs[-5:]
    cells = t0.shape[0]
    in_batches(16, copies(into(t0, ROWS), lambda at: wide[at], cells))
    if split:
        in_batches(16, copies(into(other, ROWS), lambda at: wide[at], cells, cells))
    in_batches(16, copies(into(coefs, ROWS), lambda at: coefs_own[at], COEF_ROWS * TILES))
    even = is_even(parities[0])
    blocks = ordered(block_one, block_two, even)
    sides = [ordered(one, two, even) for one, two in zip(halves(strips_one), halves(strips_two))]
    even = is_even(parities[1])
    for part, top in ((0, 0), (1, 2 * ROWS)):
        from_one, from_two = sides[0][part], sides[1][part]
        left_of = lambda at: jnp.where(even, from_two(at), from_one(at))
        right_of = lambda at: jnp.where(even, from_one(at), from_two(at))
        spread_state(
            whole,
            blocks[part],
            left_of,
            right_of,
            lambda v, a: (into(t0 if v < vectors else other, top), (2 * (v % vectors) + a) * TILES),
        )
        spread(whole, blocks[part], left_of, right_of, into(coefs, top))
    time_step(half, width, coefs, probe, (t0, t1, t2, t3), products, put_state(state))
    rows[...] = add_row(half, whole, 0, None, products)


def second_kernel(half, whole, width, t0, coefs, probe, rows_in, state, rows, t1, t2, t3, products):
    time_step(half, width, coefs, probe, (t0, t1, t2, t3), products, put_state(state))
    rows[...] = add_row(half, whole, 0, rows_in, products)


def gather_rows(first, own, one, two, parities):
    above, below = ordered(one, two, is_even(parities[0]))
    for top, read in ((0, above), (ROWS, lambda at: own[at]), (2 * ROWS, below)):
        in_batches(12, copies(into(first, top), read, first.shape[0]))


def middle_kernel(
    half, whole, width, step, own, one, two, coefs, probe, parities, rows_in, state, rows, t0, t1, t2, t3, products
):
    gather_rows(t0, own, one, two, parities)
    time_step(half, width, coefs, probe, (t0, t1, t2, t3), products, put_state(state))
    rows[...] = add_row(half, whole, step, rows_in, products)


def close_kernel(half, whole, width, own, one, two, coefs, probe, parities, rows_in, state, rows, t0, t1, t2, t3, products):
    gather_rows(t0, own, one, two, parities)
    time_step(half, width, coefs, probe, (t0, t1, t2, t3), products, put_cells(state, 0))
    rows[...] = add_row(half, whole, STEPS - 1, rows_in, products)


def last_kernel(half, whole, width, own, one, two, coefs, probe, parities, rows_in, *refs):
    state, sent, t0, t1, t2, t3, products = refs[-7:]
    gather_rows(t0, own, one, two, parities)
    for done in refs[:-7]:
        places = [(c, v, a) for c in range(2) for v in range(done.shape[1]) for a in range(2)]
        in_batches(16, [lambda at=at: [(into(state), at, done[at])] for at in places])
    time_step(half, width, coefs, probe, (t0, t1, t2, t3), products, put_cells(state, half[1]))
    rows = add_row(half, whole, STEPS - 1, rows_in, products)
    for copy in range(sent.shape[0]):
        sent[copy] = rows


def call(kernel, out_shapes, scratch=(), scalars=None, operands=0):
    in_memory = pl.BlockSpec(memory_space=pltpu.VMEM)
    specs = [pl.BlockSpec(memory_space=pltpu.SMEM) if i == scalars else in_memory for i in range(operands)]
    return pl.pallas_call(
        kernel,
        out_shape=[jax.ShapeDtypeStruct(shape, jnp.float32) for shape in out_shapes],
        in_specs=specs,
        scratch_shapes=[pltpu.VMEM(shape, jnp.float32) for shape in scratch],
        compiler_params=pltpu.CompilerParams(vmem_limit_bytes=VMEM_LIMIT),
    )


def pairings(axis):
    count = lax.axis_size(axis)
    one = [(i, i + 1 - 2 * (i % 2)) for i in range(count)]
    two = [(i, (i - 1 + 2 * (i % 2)) % count) for i in range(count)]
    return one, two


def swap(block, axis):
    one, two = pairings(axis)
    return lax.ppermute(block, axis, one), lax.ppermute(block, axis, two)


def sum_kernel(vectors, norm, rows, result):
    total = rows[0]
    for i in range(1, rows.shape[0]):
        total = total + rows[i]
    total = total * norm
    result[:, 0, :] = total[:, :vectors]
    result[:, 1, :] = total[:, vectors : 2 * vectors]


def per_device(start, probe, offsets, orbitals, index, kinds, hop_table, onsite_table):
    whole = start.shape[1]
    slots = offsets.shape[0]
    vectors = whole // PARTS
    width = 4
    groups = [(vectors, vectors * g) for g in range(PARTS)]
    cells = 2 * vectors * TILES
    edge_tiles = whole + (KINDS + 3) // 4
    tile = (ROWS, LANES)
    rows_shape = (STEPS, LANES)
    region = (cells, REGION, LANES)
    scratch = [region] * APPLY + [(2 * vectors, *tile)]
    parities = jnp.stack([lax.axis_index("gx") % 2, lax.axis_index("gy") % 2]).astype(jnp.int32)

    in_hbm = pl.BlockSpec(memory_space=pltpu.HBM)
    in_smem = pl.BlockSpec(memory_space=pltpu.SMEM)
    probe, state, coef, pair_one, pair_two = pl.pallas_call(
        functools.partial(pack_kernel, whole, slots),
        out_shape=[
            jax.ShapeDtypeStruct(shape, jnp.float32)
            for shape in (probe.shape, start.shape, (KINDS, *tile), (edge_tiles, *tile), (edge_tiles, *tile))
        ],
        in_specs=[in_hbm] * 6 + [in_smem] * 2,
        scratch_shapes=[
            pltpu.VMEM(offsets.shape, jnp.int32),
            pltpu.VMEM(index.shape, jnp.int32),
            pltpu.VMEM(kinds.shape, jnp.int32),
            pltpu.VMEM((1, hop_table.shape[0]), jnp.float32),
            pltpu.SemaphoreType.DMA((6,)),
        ],
        compiler_params=pltpu.CompilerParams(vmem_limit_bytes=VMEM_LIMIT),
    )(
        *(
            pltpu.with_memory_space_constraint(array, pltpu.HBM)
            for array in (start, probe, offsets, index, kinds, hop_table[None])
        ),
        onsite_table,
        parities,
    )
    one, two = pairings("gy")
    strips = jnp.concatenate([lax.ppermute(pair_one, "gy", one), lax.ppermute(pair_two, "gy", two)])
    (block,) = call(functools.partial(block_kernel, whole), [(4 * whole + KINDS, *tile)], operands=2)(state, coef)
    block_one, block_two = swap(block, "gx")
    strips_one, strips_two = swap(strips, "gx")
    wide, coefs_own = call(
        functools.partial(own_kernel, whole),
        [(2 * whole * TILES, *tile), (COEF_ROWS * TILES, *tile)],
        scalars=2,
        operands=3,
    )(block, strips, parities)

    state_shape = (cells, *tile)
    others = [region] * (PARTS - 1)
    first, coefs, *others, rows = call(
        functools.partial(first_kernel, groups[0], whole, width),
        [state_shape, (COEF_ROWS * TILES, REGION, LANES), *others, rows_shape],
        scratch,
        scalars=7,
        operands=8,
    )(wide, coefs_own, block_one, block_two, strips_one, strips_two, probe, parities)
    states = [first]
    for g, other in enumerate(others, 1):
        state, rows = call(
            functools.partial(second_kernel, groups[g], whole, width), [state_shape, rows_shape], scratch[1:], operands=4
        )(other, coefs, probe, rows)
        states.append(state)
    for step in range(1, STEPS - 1):
        for g in range(PARTS):
            states[g], rows = call(
                functools.partial(middle_kernel, groups[g], whole, width, step),
                [state_shape, rows_shape],
                scratch,
                scalars=5,
                operands=7,
            )(states[g], *swap(states[g], "gx"), coefs, probe, parities, rows)
    done = []
    for g in range(PARTS - 1):
        state, rows = call(
            functools.partial(close_kernel, groups[g], whole, width),
            [(2, vectors, *start.shape[2:]), rows_shape],
            scratch,
            scalars=5,
            operands=7,
        )(states[g], *swap(states[g], "gx"), coefs, probe, parities, rows)
        done.append(state)
    final, copies = call(
        functools.partial(last_kernel, groups[-1], whole, width),
        [start.shape, (lax.axis_size("gx"), *rows_shape)],
        scratch,
        scalars=5,
        operands=7 + len(done),
    )(states[-1], *swap(states[-1], "gx"), coefs, probe, parities, rows, *done)
    part = jnp.sum(lax.all_to_all(copies, "gx", 0, 0), axis=0)
    count = lax.axis_size("gy")
    copies = jnp.broadcast_to(part[None], (count, *rows_shape))
    total_cells = start.shape[3] * start.shape[4] * lax.axis_size("gx") * count
    norm = 1.0 / math.sqrt(2.0 * 2 * total_cells)
    (intersections,) = call(functools.partial(sum_kernel, whole, norm), [(STEPS, 2, whole)], operands=1)(
        lax.all_to_all(copies, "gy", 0, 0)
    )
    return final, intersections


def solution(mesh):
    return jax.shard_map(
        per_device,
        mesh=mesh,
        in_specs=(
            P(None, None, None, "gx", "gy"),
            P(None, None, None, "gx", "gy"),
            P(None, None, "gx", "gy"),
            P(None, None, "gx", "gy"),
            P(None, None, "gx", "gy"),
            P(None, "gx", "gy"),
            P(),
            P(),
        ),
        out_specs=(P(None, None, None, "gx", "gy"), P()),
        check_vma=False,
    )
```

```python
import functools
import math

import jax
import jax.numpy as jnp
from jax import lax
from jax.experimental import pallas as pl
from jax.experimental.pallas import tpu as pltpu
from jax.sharding import PartitionSpec as P

APPLY = 4
STEPS = 4
TIME_STEP = 2.6

ROWS = 8
LANES = 128
EDGE = 32
REGION = 3 * ROWS
TILES = 3
PARTS = 2
VMEM_LIMIT = 48 * 1024 * 1024

HALF = [(p, q) for p in range(3) for q in range(-2, 3) if p > 0 or q > 0]
CROSS = 2 * len(HALF)
ONSITE = CROSS + 1
KINDS = ONSITE + 2
SHIFTED = [(number, half) for number, half in enumerate(HALF) if half[1] != 0]
SHIFT_SLOT = {half: 2 * place for place, (_, half) in enumerate(SHIFTED)}
COEF_ROWS = KINDS + 2 * len(SHIFTED)


def bessel(order, arg):
    total = 0.0
    for term in range(40):
        total += (
            (-1.0) ** term
            * (arg / 2.0) ** (2 * term + order)
            / (math.factorial(term) * math.factorial(term + order))
        )
    return total


def roll(tile, amount):
    amount = amount % LANES
    return tile if amount == 0 else pltpu.roll(tile, amount, 1)


def lane_ids():
    return lax.broadcasted_iota(jnp.int32, (ROWS, LANES), 1)


def shift_tiles(tiles, amount, lanes):
    even, odd, tail = (roll(tile, amount) for tile in tiles)
    if amount > 0:
        tail = jnp.where(lanes < amount, even, tail)
        tail = jnp.where((lanes >= 64) & (lanes < 64 + amount), odd, tail)
    else:
        even = jnp.where(lanes >= LANES + amount, tail, even)
        odd = jnp.where((lanes >= 64 + amount) & (lanes < 64), tail, odd)
    return even, odd, tail


def in_batches(size, jobs):
    jobs = list(jobs)
    for start in range(0, len(jobs), size):
        triples = [triple for job in jobs[start : start + size] for triple in job()]
        for store, place, value in triples:
            store(place, value)


def into(ref, rows=None):
    def store(place, value):
        if rows is None:
            ref[place] = value
        else:
            ref[place, pl.ds(rows, ROWS), :] = value

    return store


def copies(store, read, count, shift=0):
    return [lambda at=at: [(store, at, read(at + shift))] for at in range(count)]


def in_group(lanes, group):
    return (lanes >= EDGE * group) & (lanes < EDGE * (group + 1))


def turned(real, imag):
    return roll(real, EDGE), roll(imag, EDGE + 64)


def fetch(pairs, semaphores):
    copies = [pltpu.make_async_copy(source, target, semaphores.at[i]) for i, (source, target) in enumerate(pairs)]
    for copy in copies:
        copy.start()
    for copy in copies:
        copy.wait()


def wide_table(entries):
    spare = jnp.zeros((1, LANES - entries.shape[1]), jnp.float32)
    return jnp.broadcast_to(jnp.concatenate([entries, spare], axis=1), (ROWS, LANES))


def pack_kernel(
    vectors, slots, start, probe, offsets, index, kinds, hop_table, onsite_table, parities,
    probe_copy, state, coef, pair_one, pair_two, offsets_here, index_here, kinds_here, table_here, levels_here, semaphores,
):
    fetch(
        [
            (start, state), (offsets, offsets_here), (index, index_here), (kinds, kinds_here),
            (hop_table, table_here), (onsite_table, levels_here), (probe, probe_copy),
        ],
        semaphores,
    )
    lanes = lane_ids()
    even = is_even(parities[1])

    def send(at, to_right, to_left):
        return [
            (into(pair_one), at, jnp.where(even, to_right, to_left)),
            (into(pair_two), at, jnp.where(even, to_left, to_right)),
        ]

    low = lanes < 64
    first = in_group(lanes, 0) | in_group(lanes, 2)

    def strip(v):
        strips = []
        for a in range(2):
            real, imag = turned(state[0, v, a], state[1, v, a])
            strips.append(jnp.where(low, real, imag))
        to_right = jnp.where(first, strips[0], roll(strips[1], EDGE))
        to_left = jnp.where(first, roll(strips[1], -EDGE), strips[0])
        return send(v, to_right, to_left)

    in_batches(vectors, [functools.partial(strip, v) for v in range(vectors)])
    table = wide_table(table_here[...])
    levels = wide_table(levels_here[...])
    arrays = [jnp.zeros((ROWS, LANES), jnp.float32) for _ in range(KINDS)]
    for a in range(2):
        for slot in range(slots):
            amount = jnp.take_along_axis(table, index_here[slot, a], axis=1)
            code = offsets_here[slot, a]
            for number, (p, q) in enumerate(HALF):
                at = 2 * number + a
                arrays[at] = arrays[at] + jnp.where(code == 5 * (p + 2) + q + 2, amount, 0.0)
            if a == 0:
                arrays[CROSS] = arrays[CROSS] + jnp.where(code == 12, amount, 0.0)
        arrays[ONSITE + a] = jnp.take_along_axis(levels, kinds_here[a], axis=1)
    for start_at in range(0, KINDS, 4):
        right = left = None
        for group in range(min(4, KINDS - start_at)):
            double = 2.0 * arrays[start_at + group]
            coef[start_at + group] = double
            base = roll(double, EDGE)
            from_tail = roll(base, EDGE * group)
            from_head = roll(base, EDGE * (group - 1))
            right = from_tail if right is None else jnp.where(in_group(lanes, group), from_tail, right)
            left = from_head if left is None else jnp.where(in_group(lanes, group), from_head, left)
        for store, place, value in send(vectors + start_at // 4, right, left):
            store(place, value)


def is_even(parity):
    return jnp.full((ROWS, LANES), parity, jnp.int32) == 0


def ordered(one, two, even):
    return (
        lambda at: jnp.where(even, two[at], one[at]),
        lambda at: jnp.where(even, one[at], two[at]),
    )


def widen_state(read, left_of, right_of, v, a, lanes):
    real, imag = turned(read(4 * v + 2 * a), read(4 * v + 2 * a + 1))
    left = roll(left_of(v), -EDGE * a)
    right = roll(right_of(v), EDGE * a)
    first, third = in_group(lanes, 0), in_group(lanes, 2)
    return (
        jnp.where(first, left, real),
        jnp.where(third, left, imag),
        jnp.where(first, real, jnp.where(third, imag, right)),
    )


def widen_coef(vectors, read, left_of, right_of, j, lanes):
    group = j % 4
    body = roll(read(4 * vectors + j), EDGE)
    left = roll(left_of(vectors + j // 4), -EDGE * group)
    right = roll(right_of(vectors + j // 4), EDGE * (1 - group))
    first = in_group(lanes, 0)
    even = jnp.where(first, left, body)
    tail = jnp.where(first, body, right)
    return even, roll(even, 64), jnp.where(lanes < 64, tail, roll(tail, 64))


def spread(vectors, read, left_of, right_of, store):
    lanes = lane_ids()

    def job(j):
        tiles = widen_coef(vectors, read, left_of, right_of, j, lanes)
        result = [(store, TILES * j + t, tiles[t]) for t in range(TILES)]
        if j < CROSS and HALF[j // 2][1] != 0:
            moved = shift_tiles(tiles, HALF[j // 2][1], lanes)
            at = KINDS + SHIFT_SLOT[HALF[j // 2]] + j % 2
            result += [(store, TILES * at + t, moved[t]) for t in range(TILES)]
        return result

    in_batches(4, [functools.partial(job, j) for j in range(KINDS)])


def spread_state(vectors, read, left_of, right_of, store_of):
    lanes = lane_ids()

    def job(v, a):
        store, place = store_of(v, a)
        tiles = widen_state(read, left_of, right_of, v, a, lanes)
        return [(store, place + t, tiles[t]) for t in range(TILES)]

    in_batches(4, [functools.partial(job, v, a) for v in range(vectors) for a in range(2)])


def block_kernel(vectors, state, coef, block):
    in_batches(
        16, [lambda v=v, a=a, c=c: [(into(block), 4 * v + 2 * a + c, state[c, v, a])] for v in range(vectors) for a in range(2) for c in range(2)]
    )
    in_batches(16, [lambda j=j: [(into(block), 4 * vectors + j, coef[j])] for j in range(KINDS)])


def own_kernel(vectors, block, strips, wide, coefs):
    edge = strips.shape[0] // 2
    left_of, right_of = lambda at: strips[at], lambda at: strips[edge + at]
    read = lambda at: block[at]
    spread_state(vectors, read, left_of, right_of, lambda v, a: (into(wide), (2 * v + a) * TILES))
    spread(vectors, read, left_of, right_of, into(coefs))


def coefficient(coefs, dx, dy, a, t, top):
    source = a if (dx + dy) % 2 else 1 - a
    if (dx, dy) == (0, 0):
        at, row = CROSS, top
    elif (dx, dy) in HALF:
        at = KINDS + SHIFT_SLOT[(dx, dy)] + a if dy else 2 * HALF.index((dx, dy)) + a
        row = top
    else:
        at, row = 2 * HALF.index((-dx, -dy)) + source, top + dx
    return source, coefs[TILES * at + t, pl.ds(row, ROWS), :]


def apply_twice(field, coefs, a, group, width, top, lanes):
    sums = [[[None] * 5 for _ in range(TILES)] for _ in range(width)]
    for dx in range(-2, 3):
        rows = pl.ds(top + dx, ROWS)
        for t in range(TILES):
            values = [
                [field[((group * width + w) * 2 + b) * TILES + t, rows, :] for b in range(2)]
                for w in range(width)
            ]
            for dy in range(-2, 3):
                source, factor = coefficient(coefs, dx, dy, a, t, top)
                for w in range(width):
                    term = factor * values[w][source]
                    old = sums[w][t][dy + 2]
                    sums[w][t][dy + 2] = term if old is None else old + term
            if dx == 0:
                factor = coefs[TILES * (ONSITE + a) + t, pl.ds(top, ROWS), :]
                for w in range(width):
                    sums[w][t][2] = sums[w][t][2] + factor * values[w][a]
    results = []
    for w in range(width):
        total = [sums[w][t][2] for t in range(TILES)]
        for dy in (-2, -1, 1, 2):
            moved = shift_tiles([sums[w][t][dy + 2] for t in range(TILES)], -dy, lanes)
            total = [total[t] + moved[t] for t in range(TILES)]
        results.append(total)
    return results


def time_step(half, width, coefs, probe, terms, products, finish):
    vectors, start = half
    lanes = lane_ids()
    scale = [bessel(order, TIME_STEP) * (1.0 if order == 0 else 2.0) for order in range(APPLY + 1)]
    for order in range(1, APPLY + 1):
        low, high = 2 * order, REGION - 2 * order
        tops = list(range(low, high - ROWS + 1, ROWS))
        if tops[-1] != high - ROWS:
            tops.append(high - ROWS)
        for a in range(2):

            def body(group, carry):
                for top in tops:
                    images = apply_twice(terms[order - 1], coefs, a, group, width, top, lanes)
                    stores = []
                    for w in range(width):
                        v = group * width + w
                        at = (2 * v + a) * TILES
                        rows = pl.ds(top, ROWS)
                        if order == 1:
                            new = [0.5 * images[w][t] for t in range(TILES)]
                        else:
                            new = [images[w][t] - terms[order - 2][at + t, rows, :] for t in range(TILES)]
                        if order < APPLY:
                            stores += [(into(terms[order], top), at + t, new[t]) for t in range(TILES)]
                            continue
                        even = []
                        odd = []
                        for t in range(TILES):
                            part = [terms[k][at + t, rows, :] for k in range(APPLY)]
                            even.append(scale[0] * part[0] - scale[2] * part[2] + scale[4] * new[t])
                            odd.append(roll(scale[1] * part[1] - scale[3] * part[3], 64))
                        real = even[0] + odd[1]
                        imag = even[1] - odd[0]
                        tail = even[2] + jnp.where(lanes < 64, odd[2], -odd[2])
                        own_real = roll(jnp.where(in_group(lanes, 0), tail, real), -EDGE)
                        own_imag = roll(jnp.where(in_group(lanes, 2), tail, imag), -EDGE - 64)
                        probe_real, probe_imag = probe[0, start + v, a], probe[1, start + v, a]
                        same = probe_real * own_real + probe_imag * own_imag
                        cross = probe_real * own_imag - probe_imag * own_real
                        if a == 1:
                            same = same + products[v]
                            cross = cross + products[vectors + v]
                        stores += [(into(products), v, same), (into(products), vectors + v, cross)]
                        stores += finish(at, v, a, (real, imag, tail), (own_real, own_imag))
                    for store, place, value in stores:
                        store(place, value)
                return carry

            lax.fori_loop(0, vectors // width, body, 0)


def probe_row(half, whole, products):
    vectors, start = half
    sums = jnp.sum(jnp.sum(products[...], axis=1), axis=1, keepdims=True)
    rows = lax.broadcasted_iota(jnp.int32, (2 * vectors, LANES), 0)
    lanes = lax.broadcasted_iota(jnp.int32, (2 * vectors, LANES), 1)
    place = jnp.where(rows < vectors, start + rows, whole + start + rows - vectors)
    return jnp.sum(jnp.where(lanes == place, sums, 0.0), axis=0, keepdims=True)


def add_row(half, whole, step, rows, products):
    here = lax.broadcasted_iota(jnp.int32, (STEPS, LANES), 0) == step
    row = jnp.where(here, probe_row(half, whole, products), 0.0)
    return row if rows is None else rows[...] + row


def put_state(state):
    return lambda at, v, a, tiles, cells: [(into(state), at + t, tiles[t]) for t in range(TILES)]


def put_cells(state, start):
    return lambda at, v, a, tiles, cells: [(into(state), (c, start + v, a), cells[c]) for c in range(2)]


def first_kernel(
    half, whole, width, wide, coefs_own, block_one, block_two, strips_one, strips_two, probe, parities, *refs
):
    vectors, _ = half
    split = vectors < whole
    state, coefs = refs[:2]
    other, rows = refs[2:4] if split else (None, refs[2])
    t0, t1, t2, t3, products = refs[-5:]
    cells = t0.shape[0]
    in_batches(16, copies(into(t0, ROWS), lambda at: wide[at], cells))
    if split:
        in_batches(16, copies(into(other, ROWS), lambda at: wide[at], cells, cells))
    in_batches(16, copies(into(coefs, ROWS), lambda at: coefs_own[at], COEF_ROWS * TILES))
    even = is_even(parities[0])
    blocks = ordered(block_one, block_two, even)
    strips = ordered(strips_one, strips_two, even)
    edge = strips_one.shape[0] // 2
    for part, top in ((0, 0), (1, 2 * ROWS)):
        left_of = strips[part]
        right_of = lambda at, part=part: strips[part](edge + at)
        spread_state(
            whole,
            blocks[part],
            left_of,
            right_of,
            lambda v, a: (into(t0 if v < vectors else other, top), (2 * (v % vectors) + a) * TILES),
        )
        spread(whole, blocks[part], left_of, right_of, into(coefs, top))
    time_step(half, width, coefs, probe, (t0, t1, t2, t3), products, put_state(state))
    rows[...] = add_row(half, whole, 0, None, products)


def second_kernel(half, whole, width, t0, coefs, probe, rows_in, state, rows, t1, t2, t3, products):
    time_step(half, width, coefs, probe, (t0, t1, t2, t3), products, put_state(state))
    rows[...] = add_row(half, whole, 0, rows_in, products)


def gather_rows(first, own, one, two, parities):
    above, below = ordered(one, two, is_even(parities[0]))
    for top, read in ((0, above), (ROWS, lambda at: own[at]), (2 * ROWS, below)):
        in_batches(12, copies(into(first, top), read, first.shape[0]))


def middle_kernel(
    half, whole, width, step, own, one, two, coefs, probe, parities, rows_in, state, rows, t0, t1, t2, t3, products
):
    gather_rows(t0, own, one, two, parities)
    time_step(half, width, coefs, probe, (t0, t1, t2, t3), products, put_state(state))
    rows[...] = add_row(half, whole, step, rows_in, products)


def close_kernel(half, whole, width, own, one, two, coefs, probe, parities, rows_in, state, rows, t0, t1, t2, t3, products):
    gather_rows(t0, own, one, two, parities)
    time_step(half, width, coefs, probe, (t0, t1, t2, t3), products, put_cells(state, 0))
    rows[...] = add_row(half, whole, STEPS - 1, rows_in, products)


def last_kernel(half, whole, width, own, one, two, coefs, probe, parities, rows_in, *refs):
    state, sent, t0, t1, t2, t3, products = refs[-7:]
    gather_rows(t0, own, one, two, parities)
    for done in refs[:-7]:
        places = [(c, v, a) for c in range(2) for v in range(done.shape[1]) for a in range(2)]
        in_batches(16, [lambda at=at: [(into(state), at, done[at])] for at in places])
    time_step(half, width, coefs, probe, (t0, t1, t2, t3), products, put_cells(state, half[1]))
    rows = add_row(half, whole, STEPS - 1, rows_in, products)
    for copy in range(sent.shape[0]):
        sent[copy] = rows


def call(kernel, out_shapes, scratch=(), scalars=None, operands=0):
    in_memory = pl.BlockSpec(memory_space=pltpu.VMEM)
    specs = [pl.BlockSpec(memory_space=pltpu.SMEM) if i == scalars else in_memory for i in range(operands)]
    return pl.pallas_call(
        kernel,
        out_shape=[jax.ShapeDtypeStruct(shape, jnp.float32) for shape in out_shapes],
        in_specs=specs,
        scratch_shapes=[pltpu.VMEM(shape, jnp.float32) for shape in scratch],
        compiler_params=pltpu.CompilerParams(vmem_limit_bytes=VMEM_LIMIT),
    )


def pairings(axis):
    count = lax.axis_size(axis)
    one = [(i, i + 1 - 2 * (i % 2)) for i in range(count)]
    two = [(i, (i - 1 + 2 * (i % 2)) % count) for i in range(count)]
    return one, two


def swap(block, axis):
    one, two = pairings(axis)
    return lax.ppermute(block, axis, one), lax.ppermute(block, axis, two)


def sum_kernel(vectors, norm, rows, result):
    total = rows[0]
    for i in range(1, rows.shape[0]):
        total = total + rows[i]
    total = total * norm
    result[:, 0, :] = total[:, :vectors]
    result[:, 1, :] = total[:, vectors : 2 * vectors]


def per_device(start, probe, offsets, orbitals, index, kinds, hop_table, onsite_table):
    whole = start.shape[1]
    slots = offsets.shape[0]
    vectors = whole // PARTS
    width = 4
    groups = [(vectors, vectors * g) for g in range(PARTS)]
    cells = 2 * vectors * TILES
    edge_tiles = whole + (KINDS + 3) // 4
    tile = (ROWS, LANES)
    rows_shape = (STEPS, LANES)
    region = (cells, REGION, LANES)
    scratch = [region] * APPLY + [(2 * vectors, *tile)]
    parities = jnp.stack([lax.axis_index("gx") % 2, lax.axis_index("gy") % 2]).astype(jnp.int32)

    in_hbm = pl.BlockSpec(memory_space=pltpu.HBM)
    in_smem = pl.BlockSpec(memory_space=pltpu.SMEM)
    probe, state, coef, pair_one, pair_two = pl.pallas_call(
        functools.partial(pack_kernel, whole, slots),
        out_shape=[
            jax.ShapeDtypeStruct(shape, jnp.float32)
            for shape in (probe.shape, start.shape, (KINDS, *tile), (edge_tiles, *tile), (edge_tiles, *tile))
        ],
        in_specs=[in_hbm] * 7 + [in_smem],
        scratch_shapes=[
            pltpu.VMEM(offsets.shape, jnp.int32),
            pltpu.VMEM(index.shape, jnp.int32),
            pltpu.VMEM(kinds.shape, jnp.int32),
            pltpu.VMEM((1, hop_table.shape[0]), jnp.float32),
            pltpu.VMEM((1, onsite_table.shape[0]), jnp.float32),
            pltpu.SemaphoreType.DMA((7,)),
        ],
        compiler_params=pltpu.CompilerParams(vmem_limit_bytes=VMEM_LIMIT),
    )(
        *(
            pltpu.with_memory_space_constraint(array, pltpu.HBM)
            for array in (start, probe, offsets, index, kinds, hop_table[None], onsite_table[None])
        ),
        parities,
    )
    one, two = pairings("gy")
    side_one, side_two = lax.ppermute(pair_one, "gy", one), lax.ppermute(pair_two, "gy", two)
    even = parities[1] == 0
    strips = jnp.concatenate([jnp.where(even, side_two, side_one), jnp.where(even, side_one, side_two)])
    (block,) = call(functools.partial(block_kernel, whole), [(4 * whole + KINDS, *tile)], operands=2)(state, coef)
    block_one, block_two = swap(block, "gx")
    strips_one, strips_two = swap(strips, "gx")
    wide, coefs_own = call(
        functools.partial(own_kernel, whole),
        [(2 * whole * TILES, *tile), (COEF_ROWS * TILES, *tile)],
        operands=2,
    )(block, strips)

    state_shape = (cells, *tile)
    others = [region] * (PARTS - 1)
    first, coefs, *others, rows = call(
        functools.partial(first_kernel, groups[0], whole, width),
        [state_shape, (COEF_ROWS * TILES, REGION, LANES), *others, rows_shape],
        scratch,
        scalars=7,
        operands=8,
    )(wide, coefs_own, block_one, block_two, strips_one, strips_two, probe, parities)
    states = [first]
    for g, other in enumerate(others, 1):
        state, rows = call(
            functools.partial(second_kernel, groups[g], whole, width), [state_shape, rows_shape], scratch[1:], operands=4
        )(other, coefs, probe, rows)
        states.append(state)
    for step in range(1, STEPS - 1):
        for g in range(PARTS):
            states[g], rows = call(
                functools.partial(middle_kernel, groups[g], whole, width, step),
                [state_shape, rows_shape],
                scratch,
                scalars=5,
                operands=7,
            )(states[g], *swap(states[g], "gx"), coefs, probe, parities, rows)
    done = []
    for g in range(PARTS - 1):
        state, rows = call(
            functools.partial(close_kernel, groups[g], whole, width),
            [(2, vectors, *start.shape[2:]), rows_shape],
            scratch,
            scalars=5,
            operands=7,
        )(states[g], *swap(states[g], "gx"), coefs, probe, parities, rows)
        done.append(state)
    final, copies = call(
        functools.partial(last_kernel, groups[-1], whole, width),
        [start.shape, (lax.axis_size("gx"), *rows_shape)],
        scratch,
        scalars=5,
        operands=7 + len(done),
    )(states[-1], *swap(states[-1], "gx"), coefs, probe, parities, rows, *done)
    part = jnp.sum(lax.all_to_all(copies, "gx", 0, 0), axis=0)
    count = lax.axis_size("gy")
    copies = jnp.broadcast_to(part[None], (count, *rows_shape))
    total_cells = start.shape[3] * start.shape[4] * lax.axis_size("gx") * count
    norm = 1.0 / math.sqrt(2.0 * 2 * total_cells)
    (intersections,) = call(functools.partial(sum_kernel, whole, norm), [(STEPS, 2, whole)], operands=1)(
        lax.all_to_all(copies, "gy", 0, 0)
    )
    return final, intersections


def solution(mesh):
    return jax.shard_map(
        per_device,
        mesh=mesh,
        in_specs=(
            P(None, None, None, "gx", "gy"),
            P(None, None, None, "gx", "gy"),
            P(None, None, "gx", "gy"),
            P(None, None, "gx", "gy"),
            P(None, None, "gx", "gy"),
            P(None, "gx", "gy"),
            P(),
            P(),
        ),
        out_specs=(P(None, None, None, "gx", "gy"), P()),
        check_vma=False,
    )
```
